512 devices in a mesh: row: 32 (over z, y_hi), col: 16 (over y_lo, x, core).
Axes of the slice: x: 4, y: 4 (y_hi: 2, y_lo: 2; y = y_hi * 2 + y_lo), z: 16, core: 2. Of those that a mesh axis runs over, the one named last changes fastest.
Arguments:
- features: float32 [65536, 128], P(('row', 'col')), may hold values from -6 to 6
- weight: float32 [128, 128], replicated, may hold values from -0.5 to 0.5
- grad_out: float32 [65536, 128], P(('row', 'col')), may hold values from -6 to 6
- adj_tiles: bfloat16 [32, 16, 16, 128, 128], P('row', 'col'), may hold values from 0 to 0.2795085
- tile_rows: int32 [32, 16, 16], P('row', 'col'), may hold values from 0 to 15
- tile_cols: int32 [32, 16, 16], P('row', 'col'), may hold values from 0 to 31
- tile_count: int32 [32, 16], P('row', 'col'), may hold values from 1 to 16, as said below
Outputs:
- activated: float32 [65536, 128], P(('row', 'col'))
- grad_in: float32 [65536, 128], P(('row', 'col'))
The draws below stay inside these ranges and needn't reach their ends.
Inputs may be any that keep to these rules, and one draw needn't show every extreme that they name: `tile_count`: some device block has exactly 16 live slots.
All inputs are finite; a program needn't handle non-finite values.
Results may differ from the reference program's by a relative error of at most 0.005.
Values sent between devices are 32-bit elements; how exact they have to be, the bound alone decides.
A program may use at most 64 MiB of HBM per device.

```python
import jax
import jax.numpy as jnp
from jax import lax

F = 128
TILE = 128
NODEB = 128
TILES_MAX = 16
ROW_BLOCKS = 32
COL_BLOCKS = 16
NODES = 65536
N_ROW = 32
N_COL = 16


def draw_tile_count(key, part):
    key = jax.random.fold_in(key, 7)
    first_key, second_key = jax.random.split(key)
    levels = jax.random.randint(first_key, (ROW_BLOCKS, COL_BLOCKS), 0, 9).astype(jnp.int32)
    counts = 1 + levels * levels * (TILES_MAX - 1) // 64
    target = jax.random.randint(second_key, (), 0, ROW_BLOCKS * COL_BLOCKS)
    flat_counts = counts.reshape(-1).at[target].set(TILES_MAX)
    return flat_counts.reshape(ROW_BLOCKS, COL_BLOCKS).astype(jnp.int32)


def draw_adj_tiles(key, part):
    key = jax.random.fold_in(key, 11)
    edge_key, value_key = jax.random.split(key)
    shape = (ROW_BLOCKS, COL_BLOCKS, TILES_MAX, TILE, TILE)
    present = (jax.random.randint(edge_key, shape, 0, 16) == 0).astype(jnp.float32)
    scale = (TILES_MAX * TILE * TILE / (40.0 * NODEB)) ** (-0.5)
    values = jax.random.uniform(value_key, shape, jnp.float32, 0.5, 1.5)
    return (present * values * scale).astype(jnp.bfloat16)


def with_ends(result, stream_key, smallest, top_value):
    index_at = [jax.random.randint(jax.random.fold_in(stream_key, axis), (), 0, length) for axis, length in enumerate(result.shape)]
    longest = result.shape.index(max(result.shape))
    next_to = index_at[:longest] + [(index_at[longest] + 1) % result.shape[longest]] + index_at[longest + 1:]
    return result.at[tuple(index_at)].set(smallest).at[tuple(next_to)].set(top_value)


def shard_levels(rng, extent, pieces, least, top_value):
    def one(dim, shards_of):
        draws = jax.random.uniform(jax.random.fold_in(jax.random.fold_in(rng, 6), dim), (shards_of,), jnp.float32, least / len(pieces), top_value / len(pieces))
        return jnp.repeat(jnp.exp(draws), extent[dim] // shards_of).reshape((-1,) + (1,) * (len(extent) - dim - 1))

    loudness = one(*pieces[0])
    for cut in pieces[1:]:
        loudness = loudness * one(*cut)
    return loudness


def scatter_about(rng, extent, spread, most, cuts=(), kind=jnp.bfloat16):
    drawn = spread * jax.random.normal(rng, extent, jnp.float32)
    if cuts:
        drawn = drawn * shard_levels(rng, extent, cuts, -0.22, 0.18)
    return jnp.clip(drawn, -most, most).astype(kind)


def setup_inputs(seed: int = 0) -> dict:
    key_of = jax.random.split(jax.random.key(seed), 8)
    features = scatter_about(key_of[0], (NODES, F), 1.0, 6.0, ((0, 512),), jnp.float32)
    weight = scatter_about(key_of[1], (F, F), F ** -0.5, 0.5, (), jnp.float32)
    grad_out = scatter_about(key_of[2], (NODES, F), 1.0, 6.0, ((0, 512),), jnp.float32)
    adj_tiles = draw_adj_tiles(jax.random.fold_in(key_of[7], 71), 0)
    tile_rows = with_ends(jax.random.randint(key_of[4], (ROW_BLOCKS, COL_BLOCKS, TILES_MAX), 0, N_COL * NODEB // TILE), jax.random.fold_in(key_of[4], 1), 0, (N_COL * NODEB // TILE) - 1).astype(jnp.int32)
    tile_cols = with_ends(jax.random.randint(key_of[5], (ROW_BLOCKS, COL_BLOCKS, TILES_MAX), 0, N_ROW * NODEB // TILE), jax.random.fold_in(key_of[5], 1), 0, (N_ROW * NODEB // TILE) - 1).astype(jnp.int32)
    tile_count = draw_tile_count(jax.random.fold_in(key_of[7], 71), 0)
    return dict(features=features, weight=weight, grad_out=grad_out, adj_tiles=adj_tiles, tile_rows=tile_rows, tile_cols=tile_cols, tile_count=tile_count)


def combine(tiles_in, take_index, put_index, live_mask, source, slot_count, transposed):
    chosen = jnp.take(source, take_index, axis=0)
    pattern = "tab,taf->tbf" if transposed else "tab,tbf->taf"
    products = jnp.einsum(pattern, tiles_in.astype(jnp.float32), chosen, precision=lax.Precision.HIGHEST)
    products = products * live_mask[:, None, None]
    one_hot = (put_index[:, None] == jnp.arange(slot_count, dtype=jnp.int32)[None, :]).astype(jnp.float32)
    return jnp.einsum("ts,taf->saf", one_hot, products, precision=lax.Precision.HIGHEST)


def reference(features, weight, grad_out, adj_tiles, tile_rows, tile_cols, tile_count):
    blocks_row = N_COL * NODEB // TILE
    blocks_col = N_ROW * NODEB // TILE
    shaped = features.reshape(N_ROW, N_COL, NODEB, F)
    slot_ids = jnp.arange(TILES_MAX, dtype=jnp.int32)

    def forward_row(row_id):
        def advance(total, col_id):
            source = shaped[:, col_id].reshape(blocks_col, TILE, F)
            live_mask = (slot_ids < tile_count[row_id, col_id]).astype(jnp.float32)
            term = combine(adj_tiles[row_id, col_id], tile_cols[row_id, col_id], tile_rows[row_id, col_id], live_mask, source, blocks_row, False)
            return total + term, None
        total, unused = lax.scan(advance, jnp.zeros((blocks_row, TILE, F), jnp.float32), jnp.arange(N_COL, dtype=jnp.int32))
        return total

    aggregated = lax.map(forward_row, jnp.arange(N_ROW, dtype=jnp.int32)).reshape(NODES, F)
    pre = jnp.dot(aggregated, weight, precision=lax.Precision.HIGHEST, preferred_element_type=jnp.float32)
    activated = jnp.maximum(pre, 0.0)
    masked = jnp.where(pre > 0.0, grad_out, 0.0)
    backed = jnp.dot(masked, weight.T, precision=lax.Precision.HIGHEST, preferred_element_type=jnp.float32)
    row_blocks = backed.reshape(N_ROW, blocks_row, TILE, F)

    def backward_col(col_id):
        def advance(total, row_id):
            live_mask = (slot_ids < tile_count[row_id, col_id]).astype(jnp.float32)
            term = combine(adj_tiles[row_id, col_id], tile_rows[row_id, col_id], tile_cols[row_id, col_id], live_mask, row_blocks[row_id], blocks_col, True)
            return total + term, None
        total, unused = lax.scan(advance, jnp.zeros((blocks_col, TILE, F), jnp.float32), jnp.arange(N_ROW, dtype=jnp.int32))
        return total

    gathered = lax.map(backward_col, jnp.arange(N_COL, dtype=jnp.int32))
    grad_in = gathered.reshape(N_COL, N_ROW, NODEB, F).transpose(1, 0, 2, 3).reshape(NODES, F)
    return activated, grad_in
```

```python
import functools

import jax
import jax.numpy as jnp
from jax import lax
from jax.experimental import pallas as pl
from jax.experimental.pallas import tpu as pltpu
from jax.sharding import PartitionSpec as P

F32 = jnp.float32
BF16 = jnp.bfloat16
MESH = pl.DeviceIdType.MESH
B = 128
SLOTS = 16
NZ = 16
CHIPS = ((1, 2), (0, 2), (1, 1), (1, 3), (0, 1), (0, 3), (1, 0), (0, 0))


def split(value, parts):
    out = []
    for _ in range(parts - 1):
        head = value.astype(BF16)
        out.append(head)
        value = value - head.astype(F32)
    out.append(value.astype(BF16))
    return out


def tile_product(tile, value, parts, transposed):
    dims = (((0,), (0,)), ((), ())) if transposed else (((1,), (0,)), ((), ()))
    total = None
    for part in reversed(split(value, parts)):
        term = lax.dot_general(tile, part, dims, preferred_element_type=F32)
        total = term if total is None else total + term
    return total


def kernel(
    feat, weight, grad_out, tiles_hbm, rows, cols, count,
    act, grad_in,
    fbuf, tiles, acc, stage, sib, outb, rin, rowbuf, snd, rsin, total1, hx,
    prev_r, prev_c, last_r, last_c,
    tile_sem, px_s, px_r, ag_s, ag_r, sb_s, sb_r, rc_s, rc_r, cg_s, cg_r, cs_s, cs_r, rs_s, rs_r, hx_s, hx_r,
):
    me_row = lax.axis_index("row")
    me_col = lax.axis_index("col")
    z, h = me_row // 2, lax.rem(me_row, 2)
    core = lax.rem(me_col, 2)
    chip = me_col // 2
    y, x = chip // 4, lax.rem(chip, 4)

    def row_id(zz, q):
        return lax.rem(zz + 2 * NZ, NZ) * 2 + (h if q == 0 else 1 - h)

    def chip_to(k):
        dy, dx = CHIPS[k]
        return (lax.rem(y + dy, 2)) * 4 + lax.rem(x + dx, 4)

    def chip_from(k):
        dy, dx = CHIPS[k]
        return (lax.rem(y + dy, 2)) * 4 + lax.rem(x + 4 - dx, 4)

    sends = []

    def send(src, dst, s_sem, r_sem, dev):
        copy = pltpu.make_async_remote_copy(
            src_ref=src, dst_ref=dst, send_sem=s_sem, recv_sem=r_sem,
            device_id=dev, device_id_type=MESH,
        )
        copy.start()
        sends.append(copy)
        return copy

    ring = ((row_id(z + 1, 0), me_col), (row_id(z - 1, 0), me_col))
    partner = (row_id(z, 1), me_col)
    sibling = (me_row, chip * 2 + 1 - core)
    peers = [(me_row, chip_to(k) * 2 + core) for k in range(7)]

    tile_copy = pltpu.make_async_copy(tiles_hbm, tiles, tile_sem)
    tile_copy.start()

    barrier = pltpu.get_barrier_semaphore()
    everyone = list(ring) + [partner, sibling] + peers
    for dev in everyone:
        pl.semaphore_signal(barrier, inc=1, device_id=dev, device_id_type=MESH)
    pl.semaphore_wait(barrier, len(everyone))

    ag = {}
    for d in range(2):
        ag[d, 0, 0] = send(feat, fbuf.at[me_row], ag_s.at[d, 0, 0], ag_r.at[d, 0, 0], ring[d])
    px = send(feat, fbuf.at[me_row], px_s, px_r, partner)
    fbuf[me_row] = feat[...]

    live = count[0]
    key_r = [jnp.where(t < live, rows[t], -1 - t) for t in range(SLOTS)]
    key_c = [jnp.where(t < live, cols[t], -1 - t) for t in range(SLOTS)]
    for t in range(SLOTS):
        pr, pc = jnp.int32(SLOTS), jnp.int32(SLOTS)
        for u in range(t):
            pr = jnp.where(key_r[u] == key_r[t], u, pr)
            pc = jnp.where(key_c[u] == key_c[t], u, pc)
        prev_r[t] = pr
        prev_c[t] = pc
    for r in range(16):
        last = jnp.int32(SLOTS)
        for t in range(SLOTS):
            last = jnp.where(key_r[t] == r, t, last)
        last_r[r] = last
    for r in range(32):
        last = jnp.int32(SLOTS)
        for t in range(SLOTS):
            last = jnp.where(key_c[t] == r, t, last)
        last_c[r] = last
    acc[SLOTS] = jnp.zeros((B, B), F32)

    for s in range(8):
        for q in range(2):
            for d in range(2):
                if (s == 0 and q == 0) or (s == 7 and q != d):
                    continue
                if s == 0 and d == 0:
                    px.wait_recv()
                if s > 0:
                    ag[d, s - 1, q].wait_recv()
                block = row_id(z - s if d == 0 else z + s, q)
                ag[d, s, q] = send(
                    fbuf.at[block], fbuf.at[block], ag_s.at[d, s, q], ag_r.at[d, s, q], ring[d]
                )
    ag[0, 6, 1].wait_recv()
    ag[1, 6, 0].wait_recv()
    ag[0, 7, 0].wait_recv()
    ag[1, 7, 1].wait_recv()

    tile_copy.wait()
    for t in range(SLOTS):
        acc[t] = tile_product(tiles[t], fbuf[cols[t]], 3, False) + acc[prev_r[t]]

    sb, rc = [], []
    for k in range(8):
        stage[k] = acc[last_r[chip_to(k) * 2 + 1 - core]]
        sb.append(send(stage.at[k], sib.at[k], sb_s.at[k], sb_r.at[k], sibling))
    for k in range(8):
        mine = acc[last_r[chip_to(k) * 2 + core]]
        sb[k].wait_recv()
        outb[k] = mine + sib[k]
        if k < 7:
            rc.append(send(outb.at[k], rin.at[k], rc_s.at[k], rc_r.at[k], peers[k]))
    aggregated = outb[7]
    for k in reversed(range(7)):
        rc[k].wait_recv()
        aggregated = aggregated + rin[k]

    pre = jnp.dot(
        aggregated, weight[...], precision=lax.Precision.HIGHEST, preferred_element_type=F32
    )
    masked = jnp.where(pre > 0.0, grad_out[...], 0.0)
    rowbuf[me_col] = lax.dot_general(
        masked, weight[...], (((1,), (1,)), ((), ())),
        precision=lax.Precision.HIGHEST, preferred_element_type=F32,
    )

    cg, cs = [], []
    own = rowbuf.at[me_col]
    for k in range(7):
        cg.append(send(own, own, cg_s.at[k], cg_r.at[k], peers[k]))
    cs.append(send(own, own, cs_s.at[7], cs_r.at[7], sibling))
    act[...] = jnp.maximum(pre, 0.0)
    for k in reversed(range(7)):
        cg[k].wait_recv()
        block = rowbuf.at[chip_from(k) * 2 + core]
        cs.append(send(block, block, cs_s.at[k], cs_r.at[k], sibling))
    for copy in cs:
        copy.wait_recv()

    for t in range(SLOTS):
        acc[t] = tile_product(tiles[t], rowbuf[rows[t]], 2, True) + acc[prev_c[t]]

    rs = {}
    for s in range(8):
        for q in (1, 0):
            for d in range(2):
                if s == 0 and q != d:
                    continue
                block = row_id(z + 8 - s if d == 0 else z - 8 + s, q)
                mine = acc[last_c[block]]
                if (d, s - 1, q) in rs:
                    rs[d, s - 1, q].wait_recv()
                    mine = mine + rsin[d, s - 1, q]
                snd[d, s, q] = mine
                rs[d, s, q] = send(
                    snd.at[d, s, q], rsin.at[d, s, q], rs_s.at[d, s, q], rs_r.at[d, s, q], ring[d]
                )
    theirs = acc[last_c[row_id(z, 1)]]
    rs[0, 7, 1].wait_recv()
    rs[1, 7, 1].wait_recv()
    total1[...] = theirs + rsin[0, 7, 1] + rsin[1, 7, 1]
    across = send(total1, hx, hx_s, hx_r, partner)
    mine = acc[last_c[row_id(z, 0)]]
    rs[0, 7, 0].wait_recv()
    rs[1, 7, 0].wait_recv()
    mine = mine + rsin[0, 7, 0] + rsin[1, 7, 0]
    across.wait_recv()
    grad_in[...] = mine + hx[...]

    for copy in sends:
        copy.wait_send()


def body(features, weight, grad_out, adj_tiles, tile_rows, tile_cols, tile_count):
    vmem = pl.BlockSpec(memory_space=pltpu.VMEM)
    smem = pl.BlockSpec(memory_space=pltpu.SMEM)
    dma = pltpu.SemaphoreType.DMA
    return pl.pallas_call(
        kernel,
        out_shape=[jax.ShapeDtypeStruct((B, B), F32)] * 2,
        in_specs=[vmem, vmem, vmem, pl.BlockSpec(memory_space=pl.ANY), smem, smem, smem],
        out_specs=[vmem, vmem],
        scratch_shapes=[
            pltpu.VMEM((32, B, B), F32),
            pltpu.VMEM((SLOTS, B, B), BF16),
            pltpu.VMEM((SLOTS + 1, B, B), F32),
            pltpu.VMEM((8, B, B), F32),
            pltpu.VMEM((8, B, B), F32),
            pltpu.VMEM((8, B, B), F32),
            pltpu.VMEM((7, B, B), F32),
            pltpu.VMEM((16, B, B), F32),
            pltpu.VMEM((2, 8, 2, B, B), F32),
            pltpu.VMEM((2, 8, 2, B, B), F32),
            pltpu.VMEM((B, B), F32),
            pltpu.VMEM((B, B), F32),
            pltpu.SMEM((SLOTS,), jnp.int32),
            pltpu.SMEM((SLOTS,), jnp.int32),
            pltpu.SMEM((16,), jnp.int32),
            pltpu.SMEM((32,), jnp.int32),
            dma(()), dma(()), dma(()),
            dma((2, 8, 2)), dma((2, 8, 2)),
            dma((8,)), dma((8,)),
            dma((7,)), dma((7,)),
            dma((7,)), dma((7,)),
            dma((8,)), dma((8,)),
            dma((2, 8, 2)), dma((2, 8, 2)),
            dma(()), dma(()),
        ],
        compiler_params=pltpu.CompilerParams(
            collective_id=0, has_side_effects=True, vmem_limit_bytes=40 * 1024 * 1024
        ),
        name="graph_layer",
    )(
        features, weight, grad_out,
        adj_tiles.reshape(SLOTS, B, B), tile_rows.reshape(SLOTS),
        tile_cols.reshape(SLOTS), tile_count.reshape(1),
    )


def solution(mesh):
    nodes = P(("row", "col"), None)
    return jax.shard_map(
        body,
        mesh=mesh,
        in_specs=(
            nodes,
            P(),
            nodes,
            P("row", "col", None, None, None),
            P("row", "col", None),
            P("row", "col", None),
            P("row", "col"),
        ),
        out_specs=(nodes, nodes),
        check_vma=False,
    )
```

```python
import functools

import jax
import jax.numpy as jnp
from jax import lax
from jax.experimental import pallas as pl
from jax.experimental.pallas import tpu as pltpu
from jax.sharding import PartitionSpec as P

F32 = jnp.float32
BF16 = jnp.bfloat16
MESH = pl.DeviceIdType.MESH
B = 128
SLOTS = 16
NZ = 16
SIGN = (1, -1)
CUT = 32
CHIPS = ((1, 2), (0, 2), (1, 1), (1, 3), (0, 1), (0, 3), (1, 0), (0, 0))


def span(t, d, dist):
    n = CUT if t else B
    return (0, n) if dist < 8 else (d * (n // 2), n // 2)


def split(value, parts):
    out = []
    for _ in range(parts - 1):
        head = value.astype(BF16)
        out.append(head)
        value = value - head.astype(F32)
    out.append(value.astype(BF16))
    return out


def two_sum(a, b):
    total = a + b
    shown = total - a
    return total, (a - (total - shown)) + (b - shown)


def tile_product(tile, value, parts, transposed):
    dims = (((0,), (0,)), ((), ())) if transposed else (((1,), (0,)), ((), ()))
    total = None
    for part in reversed(split(value, parts)):
        term = lax.dot_general(tile, part, dims, preferred_element_type=F32)
        total = term if total is None else total + term
    return total


def kernel(
    feat, weight_hbm, grad_hbm, tiles_hbm, rows_hbm, cols_hbm, count_hbm,
    act, grad_in,
    rows, cols, count, own_feat, weight, grad_out, fbuf, tiles, acc, stage, sib, outb, rin, rowbuf, snd, rsin, ysend, yrecv, total1, hx,
    prev_r, prev_c, last_r, last_c,
    in_sem, px_s, px_r, ya_s, ya_r, ag_s, ag_r, sb_s, sb_r, rc_s, rc_r, cg_s, cg_r, cs_s, cs_r, yr_s, yr_r, rs_s, rs_r, hx_s, hx_r,
):
    me_row = lax.axis_index("row")
    me_col = lax.axis_index("col")
    z, h = me_row // 2, lax.rem(me_row, 2)
    core = lax.rem(me_col, 2)
    chip = me_col // 2
    y, x = chip // 4, lax.rem(chip, 4)

    def row_id(zz, q):
        return lax.rem(zz + 2 * NZ, NZ) * 2 + (h if q == 0 else 1 - h)

    def chip_to(k):
        dy, dx = CHIPS[k]
        return (lax.rem(y + dy, 2)) * 4 + lax.rem(x + dx, 4)

    def chip_from(k):
        dy, dx = CHIPS[k]
        return (lax.rem(y + dy, 2)) * 4 + lax.rem(x + 4 - dx, 4)

    sends = []

    def send(src, dst, s_sem, r_sem, dev):
        copy = pltpu.make_async_remote_copy(
            src_ref=src, dst_ref=dst, send_sem=s_sem, recv_sem=r_sem,
            device_id=dev, device_id_type=MESH,
        )
        copy.start()
        sends.append(copy)
        return copy

    def z_dev(delta):
        return (row_id(z + delta, 0), me_col)

    partner = (row_id(z, 1), me_col)
    sibling = (me_row, chip * 2 + 1 - core)
    peers = [(me_row, chip_to(k) * 2 + core) for k in range(7)]

    own_copy = pltpu.make_async_copy(feat, own_feat, in_sem.at[0])
    tile_copy = pltpu.make_async_copy(tiles_hbm, tiles, in_sem.at[1])
    weight_copy = pltpu.make_async_copy(weight_hbm, weight, in_sem.at[2])
    grad_copy = pltpu.make_async_copy(grad_hbm, grad_out, in_sem.at[3])
    index_copies = [
        pltpu.make_async_copy(src, dst, in_sem.at[4 + k])
        for k, (src, dst) in enumerate(((rows_hbm, rows), (cols_hbm, cols), (count_hbm, count)))
    ]
    for copy in index_copies + [own_copy, tile_copy, weight_copy, grad_copy]:
        copy.start()

    barrier = pltpu.get_barrier_semaphore()
    everyone = [z_dev(step) for step in (-2, -1, 1, 2)] + [partner, sibling] + peers
    for dev in everyone:
        pl.semaphore_signal(barrier, inc=1, device_id=dev, device_id_type=MESH)
    own_copy.wait()
    weight_copy.wait()
    fbuf[me_row] = jnp.dot(
        own_feat[...], weight[...], precision=lax.Precision.HIGHEST, preferred_element_type=F32
    )
    pl.semaphore_wait(barrier, len(everyone))

    def held(dist, d, q):
        return row_id(z - SIGN[d] * dist, q)

    def along(t, d, dist, step):
        lo, rows_n = span(t, d, dist)
        block = fbuf.at[held(dist - step, d, t), pl.ds(lo, rows_n)]
        src = block
        ag[t, d, dist] = send(
            src, block, ag_s.at[t, d, dist - 1], ag_r.at[t, d, dist - 1], z_dev(SIGN[d] * step)
        )

    def onward(t, dist):
        for d in range(2):
            if dist > 0:
                ag[t, d, dist].wait_recv()
            along(t, d, dist + 2, 2)
        for d in range(2):
            along(t, d, dist + 1, 1)

    def across(d, dist):
        lo, rows_n = span(0, d, dist)
        lo, rows_n = max(lo, CUT), lo + rows_n - max(lo, CUT)
        block = fbuf.at[held(dist, d, 0), pl.ds(lo, rows_n)]
        src = block
        ya.append(send(src, block, ya_s.at[d, dist], ya_r.at[d, dist], partner))

    ag, ya = {}, []
    first = fbuf.at[me_row, pl.ds(0, CUT)]
    px = send(first, first, px_s, px_r, partner)
    onward(0, 0)
    across(0, 0)

    for copy in index_copies:
        copy.wait()
    live = count[0]
    key_r = [jnp.where(t < live, rows[t], -1 - t) for t in range(SLOTS)]
    key_c = [jnp.where(t < live, cols[t], -1 - t) for t in range(SLOTS)]
    for t in range(SLOTS):
        pr, pc = jnp.int32(SLOTS), jnp.int32(SLOTS)
        for u in range(t):
            pr = jnp.where(key_r[u] == key_r[t], u, pr)
            pc = jnp.where(key_c[u] == key_c[t], u, pc)
        prev_r[t] = pr
        prev_c[t] = pc
    for r in range(16):
        last = jnp.int32(SLOTS)
        for t in range(SLOTS):
            last = jnp.where(key_r[t] == r, t, last)
        last_r[r] = last
    for r in range(32):
        last = jnp.int32(SLOTS)
        for t in range(SLOTS):
            last = jnp.where(key_c[t] == r, t, last)
        last_c[r] = last
    acc[SLOTS] = jnp.zeros((B, B), F32)

    px.wait_recv()
    onward(1, 0)
    for dist in (2, 4, 6):
        onward(0, dist)
        for near in (dist - 1, dist):
            for d in range(2):
                if near < dist:
                    ag[0, d, near].wait_recv()
                across(d, near)
        onward(1, dist)
    for dist in (7, 8):
        for d in range(2):
            ag[0, d, dist].wait_recv()
            across(d, dist)
    for d in range(2):
        for dist in (1, 3, 5, 7, 8):
            ag[1, d, dist].wait_recv()
    for copy in ya:
        copy.wait_recv()

    tile_copy.wait()
    grad_copy.wait()
    for t in range(SLOTS):
        acc[t] = tile_product(tiles[t], fbuf[cols[t]], 3, False) + acc[prev_r[t]]

    sb, rc = [], []
    for k in range(8):
        stage[k] = acc[last_r[chip_to(k) * 2 + 1 - core]]
        sb.append(send(stage.at[k], sib.at[k], sb_s.at[k], sb_r.at[k], sibling))
    for k in range(8):
        mine = acc[last_r[chip_to(k) * 2 + core]]
        sb[k].wait_recv()
        outb[k] = mine + sib[k]
        if k < 7:
            rc.append(send(outb.at[k], rin.at[k], rc_s.at[k], rc_r.at[k], peers[k]))
    pre, rest = outb[7], jnp.zeros((B, B), F32)
    for k in reversed(range(7)):
        rc[k].wait_recv()
        pre, error = two_sum(pre, rin[k])
        rest = rest + error
    pre = pre + rest
    masked = jnp.where(pre > 0.0, grad_out[...], 0.0)
    rowbuf[me_col] = lax.dot_general(
        masked, weight[...], (((1,), (1,)), ((), ())),
        precision=lax.Precision.HIGHEST, preferred_element_type=F32,
    )

    cg, cs = [], []
    own = rowbuf.at[me_col]
    for k in range(7):
        cg.append(send(own, own, cg_s.at[k], cg_r.at[k], peers[k]))
    cs.append(send(own, own, cs_s.at[7], cs_r.at[7], sibling))
    act[...] = jnp.maximum(pre, 0.0)
    for k in reversed(range(7)):
        cg[k].wait_recv()
        block = rowbuf.at[chip_from(k) * 2 + core]
        cs.append(send(block, block, cs_s.at[k], cs_r.at[k], sibling))
    for copy in cs:
        copy.wait_recv()

    for t in range(SLOTS):
        acc[t] = tile_product(tiles[t], rowbuf[rows[t]], 2, True) + acc[prev_c[t]]

    order = [(0, 8)] + [(d, dist) for dist in range(7, 0, -1) for d in range(2)] + [(0, 0)]
    slot_of = {key: k for k, key in enumerate(order)}
    slot_of[1, 8] = 0
    yr = []
    for k, (d, dist) in enumerate(order):
        ysend[k] = acc[last_c[row_id(z + SIGN[d] * dist, 1)], pl.ds(CUT, B - CUT)]
        yr.append(send(ysend.at[k], yrecv.at[k], yr_s.at[k], yr_r.at[k], partner))

    rs, arrived = {}, set()

    def running(t, d, dist, lo, n):
        value = acc[last_c[row_id(z + SIGN[d] * dist, t)], pl.ds(lo, n)]
        if t == 0 and lo >= CUT:
            value = value + yrecv[slot_of[d, dist], pl.ds(lo - CUT, n)]
        for way in (0, 1) if dist == 0 else (d,):
            for back in (1, 2):
                key = t, way, dist + back
                if key in rs and dist % 2 == 0:
                    low, size = span(*key)
                    if low <= lo and lo + n <= low + size:
                        value = value + rsin[t, way, dist + back - 1, pl.ds(lo, n)]
        return value

    def pieces(t, d, dist):
        lo, n = span(t, d, dist)
        ends = {lo, lo + n}
        for edge in (CUT, span(t, 1, 8)[0]):
            if lo < edge < lo + n:
                ends.add(edge)
        ends = sorted(ends)
        return [(u, v - u) for u, v in zip(ends, ends[1:])]

    def await_parts(t, d, dist):
        if t == 0 and slot_of[d, dist] not in arrived:
            arrived.add(slot_of[d, dist])
            yr[slot_of[d, dist]].wait_recv()
        if dist % 2 == 0:
            for way in (0, 1) if dist == 0 else (d,):
                for back in (1, 2):
                    if dist + back <= 8:
                        rs[t, way, dist + back].wait_recv()

    for dist in (8, 7, 5, 6, 3, 4, 1, 2):
        for t in (1, 0):
            for d in range(2):
                await_parts(t, d, dist)
                for lo, n in pieces(t, d, dist):
                    snd[t, d, dist - 1, pl.ds(lo, n)] = running(t, d, dist, lo, n)
                lo, n = span(t, d, dist)
                at = t, d, dist - 1, pl.ds(lo, n)
                rs[t, d, dist] = send(
                    snd.at[at], rsin.at[at], rs_s.at[t, d, dist - 1], rs_r.at[t, d, dist - 1],
                    z_dev(SIGN[d] * (2 - dist % 2)),
                )
    await_parts(1, 0, 0)
    total1[...] = running(1, 0, 0, 0, CUT)
    last = send(total1, hx, hx_s, hx_r, partner)
    await_parts(0, 0, 0)
    grad_in[pl.ds(CUT, B - CUT)] = running(0, 0, 0, CUT, B - CUT)
    head = running(0, 0, 0, 0, CUT)
    last.wait_recv()
    grad_in[pl.ds(0, CUT)] = head + hx[...]

    for copy in sends:
        copy.wait_send()


def body(features, weight, grad_out, adj_tiles, tile_rows, tile_cols, tile_count):
    vmem = pl.BlockSpec(memory_space=pltpu.VMEM)
    dma = pltpu.SemaphoreType.DMA
    return pl.pallas_call(
        kernel,
        out_shape=[jax.ShapeDtypeStruct((B, B), F32)] * 2,
        in_specs=[pl.BlockSpec(memory_space=pl.ANY)] * 7,
        out_specs=[vmem, vmem],
        scratch_shapes=[
            pltpu.SMEM((SLOTS,), jnp.int32),
            pltpu.SMEM((SLOTS,), jnp.int32),
            pltpu.SMEM((1,), jnp.int32),
            pltpu.VMEM((B, B), F32),
            pltpu.VMEM((B, B), F32),
            pltpu.VMEM((B, B), F32),
            pltpu.VMEM((32, B, B), F32),
            pltpu.VMEM((SLOTS, B, B), BF16),
            pltpu.VMEM((SLOTS + 1, B, B), F32),
            pltpu.VMEM((8, B, B), F32),
            pltpu.VMEM((8, B, B), F32),
            pltpu.VMEM((8, B, B), F32),
            pltpu.VMEM((7, B, B), F32),
            pltpu.VMEM((16, B, B), F32),
            pltpu.VMEM((2, 2, 8, B, B), F32),
            pltpu.VMEM((2, 2, 8, B, B), F32),
            pltpu.VMEM((16, B - CUT, B), F32),
            pltpu.VMEM((16, B - CUT, B), F32),
            pltpu.VMEM((CUT, B), F32),
            pltpu.VMEM((CUT, B), F32),
            pltpu.SMEM((SLOTS,), jnp.int32),
            pltpu.SMEM((SLOTS,), jnp.int32),
            pltpu.SMEM((16,), jnp.int32),
            pltpu.SMEM((32,), jnp.int32),
            dma((7,)), dma(()), dma(()),
            dma((2, 9)), dma((2, 9)),
            dma((2, 2, 8)), dma((2, 2, 8)),
            dma((8,)), dma((8,)),
            dma((7,)), dma((7,)),
            dma((7,)), dma((7,)),
            dma((8,)), dma((8,)),
            dma((16,)), dma((16,)),
            dma((2, 2, 8)), dma((2, 2, 8)),
            dma(()), dma(()),
        ],
        compiler_params=pltpu.CompilerParams(
            collective_id=0, has_side_effects=True, vmem_limit_bytes=62 * 1024 * 1024
        ),
        name="graph_layer",
    )(
        features, weight, grad_out,
        adj_tiles.reshape(SLOTS, B, B), tile_rows.reshape(SLOTS),
        tile_cols.reshape(SLOTS), tile_count.reshape(1),
    )


def solution(mesh):
    nodes = P(("row", "col"), None)
    return jax.shard_map(
        body,
        mesh=mesh,
        in_specs=(
            nodes,
            P(),
            nodes,
            P("row", "col", None, None, None),
            P("row", "col", None),
            P("row", "col", None),
            P("row", "col"),
        ),
        out_specs=(nodes, nodes),
        check_vma=False,
    )
```
